32 devices in a mesh: groups: 2 (over y), gx: 4 (over z), gy: 2 (over x), gz: 2 (over core).
Axes of the slice: x: 2, y: 2, z: 4, core: 2. Of those that a mesh axis runs over, the one named last changes fastest.
Arguments:
- positions: float32 [3, 4096], P(None, ('groups', 'gx', 'gy', 'gz')), parts along dimension 1, may hold values from 0 to 1
- atom_features: float32 [4096, 64], P(('groups', 'gx', 'gy', 'gz')), parts along dimension 0, may hold values from -6 to 6
- pair_seg: int32 [640, 128], P(('groups', 'gx', 'gy', 'gz')), parts along dimension 0, may hold values from 0 to 31
- pair_other: int32 [640, 128], P(('groups', 'gx', 'gy', 'gz')), parts along dimension 0, may hold values from -1 to 351, as said below
- send_list: int32 [1024], P(('groups', 'gx', 'gy', 'gz')), parts along dimension 0, may hold values from 0 to 127
- radial_w: float32 [2, 64, 8], replicated, may hold values from -2 to 2
- pair_wa: float32 [2, 64, 64], replicated, may hold values from -0.75 to 0.75
- pair_wb: float32 [2, 64, 64], replicated, may hold values from -0.75 to 0.75
- update_w: float32 [2, 64, 192], replicated, may hold values from -0.4375 to 0.4375
- readout: float32 [64], replicated, may hold values from -0.75 to 0.75
Outputs:
- energies: float32 [4096], P(('groups', 'gx', 'gy', 'gz')), parts along dimension 0
- forces: float32 [3, 4096], P(None, ('groups', 'gx', 'gy', 'gz')), parts along dimension 1
The draws below stay inside these ranges and needn't reach their ends.
There are 2 independent parts, one for each index of `groups`. The reference program is written for one: setup_inputs(seed, part) draws one part's arguments, and reference() takes and returns one part's arrays. A program takes and returns all parts, laid end to end along the dimension named above; an argument that names none is the same for every part. Nothing has to cross between parts.
Inputs may be any that keep to these rules, and one draw needn't show every extreme that they name: `pair_other`: -1 marks an empty pair slot; on each domain the share of used slots lies between about 45 and 100 percent.
All inputs are finite; a program needn't handle non-finite values.
Results may differ from the reference program's by a relative error of at most 0.0003.
Values sent between devices are 32-bit elements; how exact they have to be, the bound alone decides.
A program may use at most 128 MiB of HBM per device.

```python
import math
from functools import partial
import jax
import jax.numpy as jnp
import numpy as np
from jax import lax

CH = 64
BASIS = 8
LAYERS = 2
SEG = 32
ATOMS = 128
GHOST = 4
N_ATOMS = 2048
NBLK = 20
PAIR_BLOCKS = 320
SEND_ALL = 512
EXT = 352
N_GX = 4
N_GY = 2
N_GZ = 2


def draw_pair_other(key, part):
    key = jax.random.fold_in(key, 11)
    first_key, second_key, third_key = jax.random.split(key, 3)
    domains = PAIR_BLOCKS // NBLK
    density = jax.random.randint(first_key, (domains, 1, 1), 45, 101)
    ticket = jax.random.randint(second_key, (domains, NBLK, 128), 0, 100)
    partner = jax.random.randint(third_key, (domains, NBLK, 128), 0, EXT)
    picked = jnp.where(ticket < density, partner, -1)
    picked = picked.at[0, 0, 0].set(EXT - 1).at[0, 0, 1].set(-1)
    return picked.reshape(PAIR_BLOCKS, 128).astype(jnp.int32)


def touch_ends(result, stream_key, smallest, top_value):
    longest = result.shape.index(max(result.shape))
    spots = []
    for shift in (0, 1):
        where = [jax.random.randint(jax.random.fold_in(stream_key, axis), (), 0, length) for axis, length in enumerate(result.shape)]
        where[longest] = (where[longest] + shift) % result.shape[longest]
        spots.append(tuple(where))
    return result.at[spots[0]].set(smallest).at[spots[1]].set(top_value)


def shard_levels(stream_key, extent, cuts, low, top_value):
    def one(position, parts):
        heights = jax.random.uniform(jax.random.fold_in(jax.random.fold_in(stream_key, 6), position), (parts,), jnp.float32, low / len(cuts), top_value / len(cuts))
        return jnp.repeat(jnp.exp(heights), extent[position] // parts).reshape((-1,) + (1,) * (len(extent) - position - 1))

    factor_of = one(*cuts[0])
    for cut in cuts[1:]:
        factor_of = factor_of * one(*cut)
    return factor_of


def scatter_about(own_key, shape, scale, reach, cuts=(), held_as=jnp.bfloat16):
    values = scale * jax.random.normal(own_key, shape, jnp.float32)
    if cuts:
        values = values * shard_levels(own_key, shape, cuts, -0.22, 0.18)
    return jnp.clip(values, -reach, reach).astype(held_as)


def setup_inputs(seed: int = 0, part: int = 0) -> dict:
    key_list = jax.random.split(jax.random.key(seed), 11)
    part_splits = jax.random.split(jax.random.fold_in(key_list[10], part), 11)
    return {
        "positions": jnp.clip(1.0 * jax.random.uniform(part_splits[0], (3, N_ATOMS), jnp.float32) ** shard_levels(part_splits[0], (3, N_ATOMS), ((1, 16),), -0.2, 0.2), 0.0, 1.0),
        "atom_features": scatter_about(part_splits[1], (N_ATOMS, CH), 1.0, 6.0, ((0, 16),), jnp.float32),
        "pair_seg": touch_ends(jax.random.randint(part_splits[2], (PAIR_BLOCKS, 128), 0, SEG), jax.random.fold_in(part_splits[2], 1), 0, SEG - 1).astype(jnp.int32),
        "pair_other": draw_pair_other(jax.random.fold_in(jax.random.fold_in(key_list[10], part), 71), part),
        "send_list": touch_ends(jax.random.randint(part_splits[4], (SEND_ALL,), 0, ATOMS), jax.random.fold_in(part_splits[4], 1), 0, ATOMS - 1).astype(jnp.int32),
        "radial_w": scatter_about(key_list[5], (LAYERS, CH, BASIS), BASIS ** -0.5, 2.0, (), jnp.float32),
        "pair_wa": scatter_about(key_list[6], (LAYERS, CH, CH), CH ** -0.5, 0.75, (), jnp.float32),
        "pair_wb": scatter_about(key_list[7], (LAYERS, CH, CH), CH ** -0.5, 0.75, (), jnp.float32),
        "update_w": scatter_about(key_list[8], (LAYERS, CH, 3 * CH), (3 * CH) ** -0.5, 0.4375, (), jnp.float32),
        "readout": scatter_about(key_list[9], (CH,), CH ** -0.5, 0.75, (), jnp.float32),
    }


exact = lax.Precision.HIGHEST
cutoff_radius = 4.0
domain_edge = 1.0
soften_square = 0.25
basis_width = 0.5
root_two = math.sqrt(2.0)
parity_sign = np.array([1.0, -1.0, -1.0, -1.0, 1.0, 1.0, 1.0, 1.0, 1.0, 1.0])

def ghost_layout():
    listing = []
    for first in range(4):
        for second in range(4):
            for third in range(4):
                inner = 1 <= first <= 2 and 1 <= second <= 2 and (1 <= third <= 2)
                if not inner:
                    listing.append((first, second, third))
    return listing

def axis_side(padded):
    if padded == 0:
        return (-1, 1)
    if padded == 3:
        return (1, 0)
    return (0, padded - 1)

def ghost_shifts():
    return np.array([[axis_side(padded)[0] for padded in ghost_slot] for ghost_slot in ghost_layout()], np.float32) * domain_edge

def harmonics(unit_vec):
    along_x = unit_vec[:, 0]
    along_y = unit_vec[:, 1]
    along_z = unit_vec[:, 2]
    trace_third = (along_x * along_x + along_y * along_y + along_z * along_z) / 3.0
    return jnp.stack([jnp.ones_like(along_x), along_x, along_y, along_z, along_x * along_x - trace_third, along_y * along_y - trace_third, along_z * along_z - trace_third, root_two * along_x * along_y, root_two * along_x * along_z, root_two * along_y * along_z], axis=1)

def pair_weights(separation, proj_centre, proj_partner, radial):
    distance = jnp.sqrt(lax.optimization_barrier(jnp.sum(separation * separation, axis=1)) + soften_square)
    unit_vec = separation / distance[:, None]
    centres = basis_width * (jnp.arange(radial.shape[1]) + 1).astype(jnp.float32)
    scaled = (distance[:, None] - centres[None, :]) / basis_width
    basis_vals = jnp.exp(-scaled * scaled)
    scaled_dist = distance / cutoff_radius
    envelope = (1.0 - scaled_dist * scaled_dist) ** 2
    before = jnp.dot(basis_vals, radial.T, precision=exact, preferred_element_type=jnp.float32) + proj_centre + proj_partner
    return (envelope[:, None] * jax.nn.silu(before), harmonics(unit_vec))

def domain_env(pos_ext, feat_ext, seg_rows, other_rows, radial, weight_a, weight_b):
    proj_a = jnp.dot(feat_ext, weight_a.T, precision=exact, preferred_element_type=jnp.float32)
    proj_b = jnp.dot(feat_ext, weight_b.T, precision=exact, preferred_element_type=jnp.float32)
    blocks = seg_rows.shape[0]
    block_base = jnp.arange(blocks, dtype=jnp.int32) * (ATOMS - SEG) // (blocks - 1)
    centre = (block_base[:, None] + seg_rows).reshape(-1)
    live_pair = (other_rows >= 0).reshape(-1)
    partner = jnp.maximum(other_rows, 0).reshape(-1)
    separation = pos_ext[partner] - pos_ext[centre]
    weights, angular = pair_weights(separation, proj_a[centre], proj_b[partner], radial)
    weights = jnp.where(live_pair[:, None], weights, 0.0)
    contrib = (angular[:, :, None] * weights[:, None, :]).reshape(-1, 10 * CH)
    flipped = angular * jnp.asarray(parity_sign, jnp.float32)[None, :]
    mirrored = (flipped[:, :, None] * weights[:, None, :]).reshape(-1, 10 * CH)
    environment = jnp.zeros((pos_ext.shape[0], 10 * CH), jnp.float32)
    return environment.at[centre].add(contrib).at[partner].add(mirrored)

def pick_rows(source_rows, chosen):
    return source_rows[chosen]

def add_rows(target_rows, chosen, addend):
    return target_rows.at[chosen].add(addend)

def gather_ghosts(rows, send_rows):
    domains = rows.shape[0]
    columns = rows.shape[2]
    sent = jax.vmap(pick_rows)(rows, send_rows)
    lattice = sent.reshape(N_GX, N_GY, N_GZ, 2, 2, 2, GHOST, columns)
    pieces = []
    for ghost_slot in ghost_layout():
        shifts = [axis_side(padded)[0] for padded in ghost_slot]
        source = [axis_side(padded)[1] for padded in ghost_slot]
        piece_rows = lattice[:, :, :, source[0], source[1], source[2]]
        pieces.append(jnp.roll(piece_rows, (-shifts[0], -shifts[1], -shifts[2]), axis=(0, 1, 2)))
    stacked = jnp.stack(pieces, axis=3)
    return stacked.reshape(domains, len(pieces) * GHOST, columns)

def return_ghosts(ghost_part, send_rows, local_part):
    domains = ghost_part.shape[0]
    columns = ghost_part.shape[2]
    lattice = ghost_part.reshape(N_GX, N_GY, N_GZ, 56, GHOST, columns)
    totals = jnp.zeros((N_GX, N_GY, N_GZ, 2, 2, 2, GHOST, columns), jnp.float32)
    for number, ghost_slot in enumerate(ghost_layout()):
        shifts = [axis_side(padded)[0] for padded in ghost_slot]
        source = [axis_side(padded)[1] for padded in ghost_slot]
        moved = jnp.roll(lattice[:, :, :, number], (shifts[0], shifts[1], shifts[2]), axis=(0, 1, 2))
        totals = totals.at[:, :, :, source[0], source[1], source[2]].add(moved)
    totals = totals.reshape(domains, 8 * GHOST, columns)
    return jax.vmap(add_rows)(local_part, send_rows, totals)

def update(features, environment, weight):
    shaped = environment.reshape(environment.shape[:-1] + (10, CH))
    scalars = 0.25 * shaped[..., 0, :]
    vectors = 0.1 * lax.optimization_barrier(jnp.sum(shaped[..., 1:4, :] * shaped[..., 1:4, :], axis=-2))
    tensors = 0.1 * lax.optimization_barrier(jnp.sum(shaped[..., 4:, :] * shaped[..., 4:, :], axis=-2))
    joined = jnp.concatenate([scalars, vectors, tensors], axis=-1)
    return features + jax.nn.silu(jnp.dot(joined, weight.T, precision=exact, preferred_element_type=jnp.float32))

def atom_energies(positions, atom_features, pair_seg, pair_other, send_list, radial_w, pair_wa, pair_wb, update_w, readout):
    domains = N_GX * N_GY * N_GZ
    own_pos = positions.T.reshape(domains, ATOMS, 3)
    features = atom_features.reshape(domains, ATOMS, CH)
    seg_blocks = pair_seg.reshape(domains, -1, 128)
    others = pair_other.reshape(domains, -1, 128)
    send_rows = send_list.reshape(domains, 8 * GHOST)
    shift_rows = jnp.repeat(jnp.asarray(ghost_shifts(), jnp.float32), GHOST, axis=0)
    ghost_pos = gather_ghosts(own_pos, send_rows) + shift_rows[None, :, :]
    pos_ext = jnp.concatenate([own_pos, ghost_pos], axis=1)
    for layer_index in range(LAYERS):
        feat_ext = jnp.concatenate([features, gather_ghosts(features, send_rows)], axis=1)
        env_fn = jax.checkpoint(partial(domain_env, radial=radial_w[layer_index], weight_a=pair_wa[layer_index], weight_b=pair_wb[layer_index]))

        def mapped(entries):
            return env_fn(entries[0], entries[1], entries[2], entries[3])
        environment = lax.map(mapped, (pos_ext, feat_ext, seg_blocks, others))
        complete = return_ghosts(environment[:, ATOMS:], send_rows, environment[:, :ATOMS])
        features = update(features, complete, update_w[layer_index])
    return jnp.dot(features, readout, precision=exact, preferred_element_type=jnp.float32).reshape(-1)

def reference(positions, atom_features, pair_seg, pair_other, send_list, radial_w, pair_wa, pair_wb, update_w, readout):

    def energies_of(where):
        return atom_energies(where, atom_features, pair_seg, pair_other, send_list, radial_w, pair_wa, pair_wb, update_w, readout)
    energies, pullback = jax.vjp(energies_of, positions)
    gradient, = pullback(jnp.ones_like(energies))
    return (energies, -gradient)
```

```python
from functools import partial
import math

import jax
import jax.numpy as jnp
import numpy as np
from jax import lax
from jax.experimental import pallas as pl
from jax.experimental.pallas import tpu as pltpu
from jax.sharding import PartitionSpec as P

CH = 64
SEG = 32
ATOMS = 128
NP = 512
GPAD = 256
AXES = ("groups", "gx", "gy", "gz")
ORDER = [1, 2, 3, 0, 4, 5, 6, 7, 8, 9]
ODD = 3 * CH
WIDE = 10 * CH
ROOT2 = math.sqrt(2.0)
F32 = jnp.float32
BF16 = jnp.bfloat16
MESH_ID = pl.DeviceIdType.MESH


def axis_side(padded):
    if padded == 0:
        return (-1, 1)
    if padded == 3:
        return (1, 0)
    return (0, padded - 1)


def axis_options(size):
    if size == 2:
        return [(0, (1, 2)), (1, (0, 3))]
    return [(0, (1, 2)), (-1, (0,)), (1, (3,))]


def neighbour_groups(sizes, ghost):
    number = {}
    for p in range(4):
        for q in range(4):
            for r in range(4):
                if not (p in (1, 2) and q in (1, 2) and r in (1, 2)):
                    number[(p, q, r)] = len(number)
    groups, slots = [], []
    for ox, ps in axis_options(sizes[0]):
        for oy, qs in axis_options(sizes[1]):
            for oz, rs in axis_options(sizes[2]):
                if ox == 0 and oy == 0 and oz == 0:
                    continue
                first = len(slots) * ghost
                slots += [(p, q, r) for p in ps for q in qs for r in rs]
                groups.append(((ox, oy, oz), first, len(slots) * ghost - first))
    rows = np.full((ATOMS + GPAD,), -5, np.int32)
    rows[:ATOMS] = np.arange(ATOMS)
    shift = np.zeros((GPAD, 128), np.float32)
    pick = np.zeros((8 * ghost, GPAD), np.float32)
    for at, key in enumerate(slots):
        sides = [axis_side(t) for t in key]
        slot = (sides[0][1] * 2 + sides[1][1]) * 2 + sides[2][1]
        for g in range(ghost):
            j = at * ghost + g
            rows[ATOMS + j] = ATOMS + number[key] * ghost + g
            shift[j, CH : CH + 3] = [s[0] for s in sides]
            pick[slot * ghost + g, j] = 1.0
    tab = np.repeat(rows[:, None], 128, axis=1)
    return groups, tab, shift, pick


def split(x):
    hi = x.astype(BF16)
    return hi, (x - hi.astype(F32)).astype(BF16)


def nn(a, b):
    return jnp.dot(a, b, preferred_element_type=F32)


def nt(a, b):
    return lax.dot_general(a, b, (((1,), (1,)), ((), ())), preferred_element_type=F32)


def nn_exact(a, b):
    return jnp.dot(a, b, precision=lax.Precision.HIGHEST, preferred_element_type=F32)


def nt_exact(a, b):
    return lax.dot_general(
        a, b, (((1,), (1,)), ((), ())), precision=lax.Precision.HIGHEST, preferred_element_type=F32
    )


def sigmoid(x):
    return 1.0 / (1.0 + jnp.exp(-x))


def kernel_body(
    groups, sizes, nblk, ghost_rows,
    pos_ref, feat_ref, seg_ref, oth_ref, send_ref, rad_ref, radt_ref, wa_ref, wb_ref, uw_ref, read_ref,
    tab_ref, shift_ref, pick_ref, base_ref,
    en_ref, force_ref,
    oh, eo, do, geo, bas, bf1, bf2, lhs, con_hi, con_lo, acc_o, acc_e, acc_g, gt_hi, gt_lo, acc_b,
    x0, pospad, xext, genv, small_out, small_in, wide_out, wide_in, send_sem, recv_sem,
):
    me = [lax.axis_index(a) for a in AXES]

    def target(offset, sign):
        ids = [me[0]]
        for k in range(3):
            ids.append(lax.rem(me[k + 1] + sign * offset[k] + sizes[k], sizes[k]))
        return tuple(ids)

    barrier = pltpu.get_barrier_semaphore()
    for offset, first, count in groups:
        pl.semaphore_signal(barrier, inc=1, device_id=target(offset, 1), device_id_type=MESH_ID)

    def exchange(k, src, dst, sign):
        copies = []
        for n, (offset, first, count) in enumerate(groups):
            copies.append(
                pltpu.make_async_remote_copy(
                    src_ref=src.at[pl.ds(first, count)],
                    dst_ref=dst.at[pl.ds(first, count)],
                    send_sem=send_sem.at[k, n],
                    recv_sem=recv_sem.at[k, n],
                    device_id=target(offset, sign),
                    device_id_type=MESH_ID,
                )
            )
        for copy in copies:
            copy.start()
        return copies

    def finish(copies):
        for copy in copies:
            copy.wait()

    chunks = nblk * 128 // NP

    pospad[...] = jnp.zeros_like(pospad)
    pospad[0:3, :] = pos_ref[...]
    eye = (
        lax.broadcasted_iota(jnp.int32, (128, 128), 0) == lax.broadcasted_iota(jnp.int32, (128, 128), 1)
    ).astype(F32)
    x0[:, 0:CH] = feat_ref[...]
    x0[:, CH:128] = nt_exact(eye, pospad[...])
    slots = send_ref.shape[1]
    sot = (lax.broadcasted_iota(jnp.int32, (ATOMS, slots), 0) == send_ref[...]).astype(BF16)
    srt_f = nn(sot, pick_ref[...].astype(BF16))
    srt = srt_f.astype(BF16)
    sr = jnp.transpose(srt_f).astype(BF16)

    def pick_rows(x):
        hi, lo = split(x)
        return nn(sr, hi) + nn(sr, lo)

    def add_back(x):
        hi, lo = split(x)
        return nn(srt, hi) + nn(srt, lo)

    mid = (x0[...] - x0[...].astype(BF16).astype(F32)).astype(BF16).astype(F32)
    low = x0[...] - x0[...].astype(BF16).astype(F32) - mid
    small_out[0] = (pick_rows(x0[...]) + nn(sr, low.astype(BF16)))[:ghost_rows]
    pl.semaphore_wait(barrier, len(groups))
    moving = exchange(0, small_out.at[0], small_in.at[0], -1)

    def build(b, carry):
        other = oth_ref[pl.ds(b, 1), :]
        centre = jnp.where(other >= 0, seg_ref[pl.ds(b, 1), :] + base_ref[pl.ds(b, 1), :], -1)
        sl = pl.ds(pl.multiple_of(b * 128, 128), 128)
        c = (lax.broadcasted_iota(jnp.int32, (ATOMS, 128), 0) == centre).astype(F32)
        p = (tab_ref[...] == other).astype(F32)
        oh[0:128, sl] = c.astype(BF16)
        oh[128:512, sl] = p.astype(BF16)
        eo[:, sl] = (c + p[0:128]).astype(BF16)
        do[:, sl] = (c - p[0:128]).astype(BF16)
        return carry

    lax.fori_loop(0, nblk, build, 0)
    finish(moving)

    sign_row = jnp.where(lax.broadcasted_iota(jnp.int32, (1, WIDE), 1) < ODD, -1.0, 1.0)
    pad_rows = GPAD - ghost_rows

    def fill_ext(own, ghosts, with_shift):
        xext[0:ATOMS, :] = own
        if with_shift:
            xext[ATOMS : ATOMS + ghost_rows, :] = ghosts + shift_ref[0:ghost_rows, :]
        else:
            xext[ATOMS : ATOMS + ghost_rows, :] = ghosts
        xext[ATOMS + ghost_rows :, :] = jnp.zeros((pad_rows, 128), F32)

    def make_lhs(layer):
        feats = xext[:, 0:CH]
        pa = nt_exact(wa_ref[layer], feats[0:ATOMS])
        pb = nt_exact(wb_ref[layer], feats)
        hi, lo = split(jnp.concatenate([pa, pb], axis=1))
        lhs[0:CH, :] = hi
        lhs[CH : 2 * CH, :] = lo
        if layer == 0:
            pick = (
                lax.broadcasted_iota(jnp.int32, (16, 128), 0) + CH
                == lax.broadcasted_iota(jnp.int32, (16, 128), 1)
            ) & (lax.broadcasted_iota(jnp.int32, (16, 128), 0) < 3)
            pt = nt_exact(pick.astype(F32), xext[...])
            both = jnp.concatenate([-pt[:, 0:ATOMS], pt], axis=1)
            p1 = both.astype(BF16)
            rest = both - p1.astype(F32)
            p2, p3 = split(rest)
            lhs[128:144, :] = p1
            lhs[144:160, :] = p2
            lhs[160:176, :] = p3

    def angular(ux, uy, uz):
        third = (ux * ux + uy * uy + uz * uz) * (1.0 / 3.0)
        return [
            None, ux, uy, uz, ux * ux - third, uy * uy - third, uz * uz - third,
            ROOT2 * ux * uy, ROOT2 * ux * uz, ROOT2 * uy * uz,
        ]

    def centres():
        return 0.5 * (lax.broadcasted_iota(jnp.int32, (8, 1), 0) + 1).astype(F32)

    def forward(layer, before_ref):
        acc_o[...] = jnp.zeros_like(acc_o)
        acc_e[...] = jnp.zeros_like(acc_e)
        acc_g[...] = jnp.zeros_like(acc_g)

        def chunk(i, carry):
            sl = pl.ds(pl.multiple_of(i * NP, NP), NP)
            cp = oh[:, sl]
            if layer == 0:
                got = nn(lhs[...], cp)
                sep = got[128:136] + got[144:152] + got[160:168]
                sx, sy, sz = sep[0:1], sep[1:2], sep[2:3]
                dist = jnp.sqrt(sx * sx + sy * sy + sz * sz + 0.25)
                inv = 1.0 / dist
                ux, uy, uz = sx * inv, sy * inv, sz * inv
                scaled = dist * 0.25
                fall = 1.0 - scaled * scaled
                envelope = fall * fall
                geo[0:1, sl] = ux
                geo[1:2, sl] = uy
                geo[2:3, sl] = uz
                geo[3:4, sl] = dist
                geo[4:5, sl] = inv
                geo[5:6, sl] = envelope
                geo[6:7, sl] = -scaled * fall
                step = (dist - centres()) * 2.0
                basis = jnp.exp(-step * step)
                bas[:, sl] = basis
            else:
                got = nn(lhs[0:128, :], cp)
                ux, uy, uz = geo[0:1, sl], geo[1:2, sl], geo[2:3, sl]
                envelope = geo[5:6, sl]
                basis = bas[:, sl]
            before = nn_exact(rad_ref[layer], basis) + got[0:CH] + got[CH : 2 * CH]
            before_ref[:, sl] = before
            weight = envelope * (before * sigmoid(before))
            ang = angular(ux, uy, uz)
            for at, m in enumerate(ORDER):
                value = weight if m == 0 else weight * ang[m]
                hi, lo = split(value)
                con_hi[at * CH : (at + 1) * CH, :] = hi
                con_lo[at * CH : (at + 1) * CH, :] = lo
            d, e, g = do[:, sl], eo[:, sl], oh[256:512, sl]
            acc_o[...] += nt(d, con_hi[0:ODD]) + nt(d, con_lo[0:ODD])
            acc_e[...] += nt(e, con_hi[ODD:]) + nt(e, con_lo[ODD:])
            acc_g[...] += nt(g, con_hi[...]) + nt(g, con_lo[...])
            return carry

        lax.fori_loop(0, chunks, chunk, 0)

    def fold_env(k, w):
        wide_out[w] = (acc_g[...] * sign_row)[:ghost_rows]
        finish(exchange(k, wide_out.at[w], wide_in.at[w], 1))
        own = jnp.concatenate([acc_o[...], acc_e[...]], axis=1)
        arrived = jnp.concatenate([wide_in[w], jnp.zeros((pad_rows, WIDE), F32)], axis=0)
        return own + add_back(arrived)

    def part(env, at):
        return env[:, at * CH : (at + 1) * CH]

    def update(h, env, layer):
        square = [part(env, at) * part(env, at) for at in range(10)]
        vec = 0.1 * (square[0] + square[1] + square[2])
        ten = 0.1 * (square[4] + square[5] + square[6] + square[7] + square[8] + square[9])
        joined = jnp.concatenate([0.25 * part(env, 3), vec, ten], axis=1)
        z = nt_exact(joined, uw_ref[layer])
        return h + z * sigmoid(z), z

    def env_grad(hbar, z, env, layer):
        s = sigmoid(z)
        zbar = hbar * (s * (1.0 + z * (1.0 - s)))
        jbar = nn_exact(zbar, uw_ref[layer])
        sb = 0.25 * jbar[:, 0:CH]
        vb = 0.2 * jbar[:, CH : 2 * CH]
        tb = 0.2 * jbar[:, 2 * CH :]
        pieces = [vb * part(env, at) for at in range(3)] + [sb]
        pieces += [tb * part(env, at) for at in range(4, 10)]
        return jnp.concatenate(pieces, axis=1)

    def spread_env(k, w, grad):
        wide_out[w] = pick_rows(grad)[:ghost_rows]
        moving = exchange(k, wide_out.at[w], wide_in.at[w], -1)
        hi, lo = split(jnp.transpose(grad))
        gt_hi[:, 0:ATOMS] = hi
        gt_lo[:, 0:ATOMS] = lo
        finish(moving)
        full = jnp.concatenate([wide_in[w] * sign_row, jnp.zeros((pad_rows, WIDE), F32)], axis=0)
        hi, lo = split(jnp.transpose(full))
        gt_hi[:, ATOMS:] = hi
        gt_lo[:, ATOMS:] = lo

    def backward(layer, before_ref):
        acc_b[...] = jnp.zeros_like(acc_b)

        def chunk(i, carry):
            sl = pl.ds(pl.multiple_of(i * NP, NP), NP)
            d, e, g = do[:, sl], eo[:, sl], oh[256:512, sl]
            go = (
                nn(gt_hi[0:ODD, 0:ATOMS], d) + nn(gt_lo[0:ODD, 0:ATOMS], d)
                + nn(gt_hi[0:ODD, ATOMS:], g) + nn(gt_lo[0:ODD, ATOMS:], g)
            )
            ge = (
                nn(gt_hi[ODD:, 0:ATOMS], e) + nn(gt_lo[ODD:, 0:ATOMS], e)
                + nn(gt_hi[ODD:, ATOMS:], g) + nn(gt_lo[ODD:, ATOMS:], g)
            )
            ux, uy, uz = geo[0:1, sl], geo[1:2, sl], geo[2:3, sl]
            dist, inv, envelope, fall = geo[3:4, sl], geo[4:5, sl], geo[5:6, sl], geo[6:7, sl]
            basis = bas[:, sl]
            before = before_ref[:, sl]
            s = sigmoid(before)
            act = before * s
            weight = envelope * act
            ang = angular(ux, uy, uz)
            wbar = None
            abar = [None] * 10
            for at, m in enumerate(ORDER):
                gm = go[at * CH : (at + 1) * CH] if at < 3 else ge[(at - 3) * CH : (at - 2) * CH]
                term = gm if m == 0 else gm * ang[m]
                wbar = term if wbar is None else wbar + term
                if m:
                    abar[m] = jnp.sum(weight * gm, axis=0, keepdims=True)
            envbar = jnp.sum(wbar * act, axis=0, keepdims=True)
            bbar = envelope * wbar * (s * (1.0 + before * (1.0 - s)))
            kbar = nn_exact(radt_ref[layer], bbar)
            step = (dist - centres()) * 2.0
            dbar = jnp.sum(kbar * basis * step, axis=0, keepdims=True) * -4.0 + envbar * fall
            third = (abar[4] + abar[5] + abar[6]) * (1.0 / 3.0)
            xb = abar[1] + 2.0 * ux * (abar[4] - third) + ROOT2 * (uy * abar[7] + uz * abar[8])
            yb = abar[2] + 2.0 * uy * (abar[5] - third) + ROOT2 * (ux * abar[7] + uz * abar[9])
            zb = abar[3] + 2.0 * uz * (abar[6] - third) + ROOT2 * (ux * abar[8] + uy * abar[9])
            dbar = dbar - (xb * ux + yb * uy + zb * uz) * inv
            rx, ry, rz = xb * inv + ux * dbar, yb * inv + uy * dbar, zb * inv + uz * dbar
            r16 = jnp.concatenate([rx, ry, rz, jnp.zeros((13, NP), F32)], axis=0)
            r_hi, r_lo = split(r16)
            con_hi[128:144, :] = r_hi
            con_hi[144:160, :] = r_lo
            if layer == 1:
                b_hi, b_lo = split(bbar)
                con_hi[0:CH, :] = b_hi
                con_hi[CH : 2 * CH, :] = b_lo
            acc_b[...] += nt(oh[:, sl], con_hi[0:256, :])
            return carry

        lax.fori_loop(0, chunks, chunk, 0)

    def pos_rows():
        both = acc_b[:, 128:144] + acc_b[:, 144:160]
        return both[128:256] - both[0:128], both[256 : 256 + ghost_rows]

    fill_ext(x0[...], small_in[0], True)
    make_lhs(0)
    forward(0, bf1)
    genv[0] = fold_env(1, 0)
    h1, z1 = update(feat_ref[...], genv[0], 0)
    h1w = jnp.concatenate([h1, jnp.zeros((ATOMS, CH), F32)], axis=1)
    small_out[1] = pick_rows(h1w)[:ghost_rows]
    finish(exchange(2, small_out.at[1], small_in.at[1], -1))
    fill_ext(h1w, small_in[1], False)
    make_lhs(1)
    forward(1, bf2)
    genv[1] = fold_env(3, 1)
    h2, z2 = update(h1, genv[1], 1)
    en_ref[...] = nt_exact(read_ref[...], h2)
    hbar2 = jnp.broadcast_to(read_ref[...], (ATOMS, CH))
    spread_env(4, 2, env_grad(hbar2, z2, genv[1], 1))
    con_hi[...] = jnp.zeros_like(con_hi)
    backward(1, bf2)
    pos_own2, pos_ghost2 = pos_rows()
    ab = acc_b[:, 0:CH] + acc_b[:, CH : 2 * CH]
    hb = nn_exact(ab[128:512], wb_ref[1])
    small_out[2] = jnp.concatenate(
        [hb[ATOMS : ATOMS + ghost_rows], jnp.zeros((ghost_rows, CH), F32)], axis=1
    )
    moving = exchange(5, small_out.at[2], small_in.at[2], 1)
    own_bar = hbar2 + hb[0:ATOMS] + nn_exact(ab[0:128], wa_ref[1])
    finish(moving)
    arrived = jnp.concatenate([small_in[2], jnp.zeros((pad_rows, 128), F32)], axis=0)
    own_bar = own_bar + add_back(arrived)[:, 0:CH]
    spread_env(6, 3, env_grad(own_bar, z1, genv[0], 0))
    backward(0, bf1)
    pos_own1, pos_ghost1 = pos_rows()
    small_out[3] = jnp.concatenate(
        [pos_ghost1 + pos_ghost2, jnp.zeros((ghost_rows, 112), F32)], axis=1
    )
    finish(exchange(7, small_out.at[3], small_in.at[3], 1))
    arrived = jnp.concatenate([small_in[3], jnp.zeros((pad_rows, 128), F32)], axis=0)
    total = add_back(arrived)[:, 0:16] + pos_own1 + pos_own2
    pick16 = (
        lax.broadcasted_iota(jnp.int32, (8, 16), 0) == lax.broadcasted_iota(jnp.int32, (8, 16), 1)
    ).astype(F32)
    force_ref[...] = -nt_exact(pick16, total)[0:3]


def local(sizes, positions, feats, seg, oth, send, rad, wa, wb, uw, read):
    ghost = send.shape[0] // 8
    ghost_rows = 56 * ghost
    nblk = seg.shape[0]
    groups, tab, shift, pick = neighbour_groups(sizes, ghost)
    base = np.repeat((np.arange(nblk) * (ATOMS - SEG) // (nblk - 1)).astype(np.int32)[:, None], 128, axis=1)
    pairs = nblk * 128
    vm = pltpu.VMEM
    spec = pl.BlockSpec(memory_space=pltpu.VMEM)
    energies, forces = pl.pallas_call(
        partial(kernel_body, groups, sizes, nblk, ghost_rows),
        out_shape=(jax.ShapeDtypeStruct((1, ATOMS), F32), jax.ShapeDtypeStruct((3, ATOMS), F32)),
        in_specs=[spec] * 15,
        out_specs=(spec, spec),
        scratch_shapes=[
            vm((512, pairs), BF16),
            vm((ATOMS, pairs), BF16),
            vm((ATOMS, pairs), BF16),
            vm((8, pairs), F32),
            vm((8, pairs), F32),
            vm((CH, pairs), F32),
            vm((CH, pairs), F32),
            vm((176, 512), BF16),
            vm((WIDE, NP), BF16),
            vm((WIDE, NP), BF16),
            vm((ATOMS, ODD), F32),
            vm((ATOMS, WIDE - ODD), F32),
            vm((GPAD, WIDE), F32),
            vm((WIDE, ATOMS + GPAD), BF16),
            vm((WIDE, ATOMS + GPAD), BF16),
            vm((512, 256), F32),
            vm((ATOMS, 128), F32),
            vm((CH, ATOMS), F32),
            vm((ATOMS + GPAD, 128), F32),
            vm((2, ATOMS, WIDE), F32),
            vm((4, ghost_rows, 128), F32),
            vm((4, ghost_rows, 128), F32),
            vm((4, ghost_rows, WIDE), F32),
            vm((4, ghost_rows, WIDE), F32),
            pltpu.SemaphoreType.DMA((8, len(groups))),
            pltpu.SemaphoreType.DMA((8, len(groups))),
        ],
        compiler_params=pltpu.CompilerParams(
            collective_id=0, has_side_effects=True, vmem_limit_bytes=48 * 1024 * 1024
        ),
        name="pair_potential",
    )(
        positions, feats, seg, oth, send.reshape(1, -1), rad, jnp.swapaxes(rad, 1, 2), wa, wb, uw,
        read.reshape(1, -1), jnp.asarray(tab), jnp.asarray(shift), jnp.asarray(pick), jnp.asarray(base),
    )
    return energies.reshape(-1), forces


def solution(mesh):
    split_all = AXES
    sizes = tuple(mesh.shape[a] for a in AXES[1:])
    return jax.shard_map(
        partial(local, sizes),
        mesh=mesh,
        in_specs=(
            P(None, split_all),
            P(split_all, None),
            P(split_all, None),
            P(split_all, None),
            P(split_all),
            P(),
            P(),
            P(),
            P(),
            P(),
        ),
        out_specs=(P(split_all), P(None, split_all)),
        check_vma=False,
    )
```
